256 devices in a mesh: gx: 16 (over x, y_lo, core), gz: 16 (over y_hi, z).
Axes of the slice: x: 4, y: 4 (y_hi: 2, y_lo: 2; y = y_hi * 2 + y_lo), z: 8, core: 2. Of those that a mesh axis runs over, the one named last changes fastest.
Arguments:
- velocity: float32 [3, 1024, 32, 2048], P(None, 'gx', None, 'gz'), may hold values from -4 to 4
Outputs:
- new_velocity: float32 [3, 1024, 32, 2048], P(None, 'gx', None, 'gz')
- nonlinear: float32 [3, 1024, 32, 2048], P(None, 'gx', None, 'gz')
The draws below stay inside these ranges and needn't reach their ends.
All inputs are finite; a program needn't handle non-finite values.
Results may differ from the reference program's by a relative error of at most 0.0008.
Values sent between devices are 32-bit elements; how exact they have to be, the bound alone decides.
No kernel may reach another device: no remote copies, remote signals or barrier semaphores. Data moves between devices by JAX's collectives and lax.ppermute only.
A program may use at most 128 MiB of HBM per device.

```python
import jax
import jax.numpy as jnp
from jax import lax

NY = 32
NX = 1024
NZ = 2048
VISC = 12288


def draw_velocity(key, part):
    key = jax.random.fold_in(key, 11)
    shape = (3, NX, NY, NZ)
    return jnp.clip(jax.random.normal(key, shape, jnp.float32), -4.0, 4.0)


def setup_inputs(seed: int = 0) -> dict:
    seeds = jax.random.split(jax.random.key(seed), 2)
    return {
        "velocity": draw_velocity(jax.random.fold_in(seeds[1], 71), 0),
    }


courant = 0.1


def centred(field, axis):
    upper = jnp.roll(field, -1, axis) - jnp.roll(field, 1, axis)
    outer = jnp.roll(field, -2, axis) - jnp.roll(field, 2, axis)
    return (8.0 * upper - outer) / 12.0


def reference(velocity):
    offsets = jnp.arange(-2, 3, dtype=jnp.int32)
    wave_index = jnp.arange(NX // 2 + 1, dtype=jnp.float32)
    symbol = 1.0 + 4.0 * VISC * jnp.sin(jnp.pi * wave_index / NX) ** 2

    def one_plane(index):
        y_rows = ((index + offsets) % NY).astype(jnp.int32)
        y_window = jnp.take(velocity, y_rows, axis=2)
        centre = y_window[:, :, 2]
        grad_x = centred(centre, 1)
        grad_z = centred(centre, 2)
        grad_y = (8.0 * (y_window[:, :, 3] - y_window[:, :, 1]) - (y_window[:, :, 4] - y_window[:, :, 0])) / 12.0
        advect = centre[0][None] * grad_x + centre[1][None] * grad_y + centre[2][None] * grad_z
        laplace = jnp.roll(centre, -1, 1) - 2.0 * centre + jnp.roll(centre, 1, 1)
        rhs = centre + VISC * laplace - courant * advect
        spectrum = jnp.fft.rfft(rhs, axis=1) / symbol[None, :, None]
        solved = jnp.fft.irfft(spectrum, n=NX, axis=1)
        return solved.astype(jnp.float32), advect

    solved, advect = lax.map(one_plane, jnp.arange(NY, dtype=jnp.int32))
    return jnp.transpose(solved, (1, 2, 0, 3)), jnp.transpose(advect, (1, 2, 0, 3))
```

```python
import math

import jax
import jax.numpy as jnp
from jax import lax
from jax.experimental import pallas as pl
from jax.experimental.pallas import tpu as pltpu
from jax.sharding import PartitionSpec as P

VISC = 12288
COURANT = 0.1

HALF = 1.0 / (2.0 * VISC)
LAM = 1.0 + HALF - math.sqrt(2.0 * HALF + HALF * HALF)
GAIN = 1.0 / (1.0 + 2.0 * VISC * (1.0 - LAM))

X = 64
Y = 32
Z = 128
CHUNK = 8
CHUNKS = X // CHUNK
CHIPS = 8
PERIOD = 2 * X * CHIPS
F32 = jnp.float32
VM = pl.BlockSpec(memory_space=pltpu.VMEM)
ANY = pl.BlockSpec(memory_space=pl.ANY)


def params(mib):
    return pltpu.CompilerParams(vmem_limit_bytes=mib * 1024 * 1024)


def shape(*dims):
    return jax.ShapeDtypeStruct(dims, F32)


def lanes(rows):
    return lax.broadcasted_iota(jnp.int32, (rows, Z), 1)


def shift(a, amount):
    return pltpu.roll(a, amount % Z, 1)


def pack_kernel(v_ref, xa_ref, xb_ref, za_ref, zb_ref):
    px = lax.rem(lax.axis_index("gx"), 2)
    pz = lax.rem(lax.axis_index("gz"), 2)
    first = (1 - px) * (X - 2)
    xa_ref[...] = v_ref[:, pl.ds(first, 2)]
    xb_ref[...] = v_ref[:, pl.ds(X - 2 - first, 2)]
    slot = lanes(3 * Y) >> 1

    def body(x, carry):
        bottom, top = carry
        turned = pltpu.roll(v_ref[:, x].reshape(3 * Y, Z), 2 * x, 1)
        bottom = jnp.where(slot == x, turned, bottom)
        top = jnp.where(slot == lax.rem(x + X - 1, X), turned, top)
        return bottom, top

    zero = jnp.zeros((3 * Y, Z), F32)
    bottom, top = lax.fori_loop(0, X, body, (zero, zero), unroll=4)
    even = pz == 0
    za_ref[...] = jnp.where(even, top, bottom).reshape(3, Y, Z)
    zb_ref[...] = jnp.where(even, bottom, top).reshape(3, Y, Z)


def stencil_kernel(
    v_ref, xa_ref, xb_ref, za_ref, zb_ref, ra_ref, rb_ref,
    n_ref, u_ref, mom_ref,
    vp, nb, pb, edge, vsem, nsem, usem,
):
    def v_copy(j):
        rows = pl.ds(j * CHUNK, CHUNK)
        return pltpu.make_async_copy(v_ref.at[:, rows], vp.at[:, pl.ds(2 + j * CHUNK, CHUNK)], vsem.at[j])

    def n_copy(j):
        rows = pl.ds(j * CHUNK, CHUNK)
        return pltpu.make_async_copy(nb.at[:, rows], n_ref.at[:, rows], nsem.at[j])

    def u_copy(j):
        rows = pl.ds(j * CHUNK, CHUNK)
        return pltpu.make_async_copy(pb.at[:, rows], u_ref.at[:, rows], usem.at[j])

    for j in range(CHUNKS):
        v_copy(j).start()
    x_even = lax.rem(lax.axis_index("gx"), 2) == 0
    z_even = lax.rem(lax.axis_index("gz"), 2) == 0
    vp[:, 0:2] = jnp.where(x_even, xb_ref[...], xa_ref[...])
    vp[:, X + 2 : X + 4] = jnp.where(x_even, xa_ref[...], xb_ref[...])

    lane = lanes(3 * Y)
    even_lane = lane & 1 == 0
    own_top = jnp.where(z_even, za_ref[...], zb_ref[...])
    own_bottom = jnp.where(z_even, zb_ref[...], za_ref[...])
    high = (jnp.where(z_even, ra_ref[...], rb_ref[...]) - own_bottom).reshape(3 * Y, Z)
    low = (jnp.where(z_even, rb_ref[...], ra_ref[...]) - own_top).reshape(3 * Y, Z)
    low_two = shift(low, 2)
    at_bottom = jnp.where(even_lane, low_two - 8.0 * shift(low, 1), low_two)
    high_two = shift(high, -2)
    at_top = jnp.where(even_lane, -high_two, 8.0 * shift(high, -1) - high_two)
    early = lane & 3 < 2
    edge[0] = jnp.where(early, at_bottom, at_top)
    edge[1] = jnp.where(early, at_top, at_bottom)
    border = (lane < 2) | (lane >= Z - 2)

    def forward(x, carry):
        p, q, power = carry
        f = vp[:, x + 2]
        gx = 8.0 * (vp[:, x + 3] - vp[:, x + 1]) - (vp[:, x + 4] - vp[:, x])
        flat = f.reshape(3 * Y, Z)
        one = shift(flat, -1) - shift(flat, 1)
        fix = pltpu.roll(edge[lax.rem(x, 2)], lax.rem(2 * (X - x), Z), 1)
        gz = 8.0 * one - (shift(one, -1) + shift(one, 1)) + jnp.where(border, fix, 0.0)
        gz = gz.reshape(3, Y, Z)
        step = pltpu.roll(f, Y - 1, 1) - pltpu.roll(f, 1, 1)
        gy = 8.0 * step - (pltpu.roll(step, Y - 1, 1) + pltpu.roll(step, 1, 1))
        u = f * (1.0 / 12.0)
        n = u[0][None] * gx + u[1][None] * gy + u[2][None] * gz
        w = 2.0 * f - COURANT * n
        p = LAM * p + w
        q = q + power * w
        nb[:, x] = n
        pb[:, x] = p
        return p, q, power * LAM

    zero = jnp.zeros((3, Y, Z), F32)
    carry = (zero, zero, F32(1.0))
    v_copy(0).wait()
    for j in range(CHUNKS):
        if j + 1 < CHUNKS:
            v_copy(j + 1).wait()
        carry = lax.fori_loop(j * CHUNK, (j + 1) * CHUNK, forward, carry)
        n_copy(j).start()
    mom_ref[0] = carry[0]
    mom_ref[1] = carry[1]

    def backward(k, q, j):
        x = (j + 1) * CHUNK - 1 - k
        f = vp[:, x + 2]
        w = 2.0 * f - COURANT * nb[:, x]
        q = LAM * q
        pb[:, x] = GAIN * (pb[:, x] + q) - f
        return q + w

    q = zero
    for j in reversed(range(CHUNKS)):
        q = lax.fori_loop(0, CHUNK, lambda k, q, j=j: backward(k, q, j), q)
        u_copy(j).start()
    for j in range(CHUNKS):
        n_copy(j).wait()
        u_copy(j).wait()


def chip_kernel(own_ref, other_ref, out_ref):
    core = lax.rem(lax.axis_index("gx"), 2)
    rows = pl.ds(pl.multiple_of(core * (Y // 2), Y // 2), Y // 2)
    own_p, own_q = own_ref[0, :, rows], own_ref[1, :, rows]
    other_p, other_q = other_ref[0, :, rows], other_ref[1, :, rows]
    first = core == 0
    far = LAM**X
    p = jnp.where(first, own_p, other_p) * far + jnp.where(first, other_p, own_p)
    q = jnp.where(first, own_q, other_q) + far * jnp.where(first, other_q, own_q)
    for k in range(CHIPS):
        out_ref[k, 0] = p
        out_ref[k, 1] = q


def join_kernel(all_ref, out_ref):
    chip = lax.div(lax.axis_index("gx"), 2)
    p = jnp.zeros(all_ref.shape[2:], F32)
    q = p
    for s in range(1, CHIPS + 1):
        weight = LAM ** (2 * X * (s - 1)) / (1.0 - LAM**PERIOD)
        p = p + weight * all_ref[lax.rem(chip + CHIPS - s % CHIPS, CHIPS), 0]
        q = q + weight * all_ref[lax.rem(chip + s, CHIPS), 1]
    out_ref[0] = p
    out_ref[1] = q


def final_kernel(u_ref, in_own_ref, in_other_ref, other_ref, out_ref, ub, ob, isem, osem):
    def i_copy(j):
        rows = pl.ds(j * CHUNK, CHUNK)
        return pltpu.make_async_copy(u_ref.at[:, rows], ub.at[:, rows], isem.at[j])

    def o_copy(j):
        rows = pl.ds(j * CHUNK, CHUNK)
        return pltpu.make_async_copy(ob.at[:, rows], out_ref.at[:, rows], osem.at[j])

    for j in range(CHUNKS):
        i_copy(j).start()
    first = lax.rem(lax.axis_index("gx"), 2) == 0
    own, other = in_own_ref[...], in_other_ref[...]
    both = jnp.concatenate([jnp.where(first, own, other), jnp.where(first, other, own)], axis=2)
    far = LAM**X
    p_in = jnp.where(first, both[0], other_ref[0] + far * both[0])
    q_in = jnp.where(first, other_ref[1] + far * both[1], both[1])

    def body(x, carry):
        p, q = carry
        ob[:, x] = ub[:, x] + (p + q)
        return p * LAM, q * (1.0 / LAM)

    carry = ((GAIN * LAM) * p_in, (GAIN * far) * q_in)
    for j in range(CHUNKS):
        i_copy(j).wait()
        carry = lax.fori_loop(j * CHUNK, (j + 1) * CHUNK, body, carry)
        o_copy(j).start()
    for j in range(CHUNKS):
        o_copy(j).wait()


def pair_low(count):
    return [(i, i ^ 1) for i in range(count)]


def pair_high(count):
    return [(i, (i + 1 if i % 2 else i - 1) % count) for i in range(count)]


def shards(v):
    nx, nz = lax.axis_size("gx"), lax.axis_size("gz")
    sems = [pltpu.SemaphoreType.DMA((CHUNKS,))]
    xa, xb, za, zb = pl.pallas_call(
        pack_kernel,
        out_shape=[shape(3, 2, Y, Z)] * 2 + [shape(3, Y, Z)] * 2,
        in_specs=[VM],
        out_specs=[VM] * 4,
        compiler_params=params(16),
        name="pack",
    )(v)
    rzb = lax.ppermute(zb, "gz", pair_high(nz))
    rza = lax.ppermute(za, "gz", pair_low(nz))
    rxb = lax.ppermute(xb, "gx", pair_high(nx))
    rxa = lax.ppermute(xa, "gx", pair_low(nx))
    n, u, mom = pl.pallas_call(
        stencil_kernel,
        out_shape=[shape(3, X, Y, Z), shape(3, X, Y, Z), shape(2, 3, Y, Z)],
        in_specs=[ANY] + [VM] * 6,
        out_specs=[ANY, ANY, VM],
        scratch_shapes=[
            pltpu.VMEM((3, X + 4, Y, Z), F32),
            pltpu.VMEM((3, X, Y, Z), F32),
            pltpu.VMEM((3, X, Y, Z), F32),
            pltpu.VMEM((2, 3 * Y, Z), F32),
        ]
        + sems * 3,
        compiler_params=params(24),
        name="stencil",
    )(v, rxa, rxb, za, zb, rza, rzb)
    other = lax.ppermute(mom, "gx", pair_low(nx))
    half = (2, 3, Y // 2, Z)
    chip = pl.pallas_call(
        chip_kernel,
        out_shape=shape(CHIPS, *half),
        in_specs=[VM, VM],
        out_specs=VM,
        compiler_params=params(16),
        name="chip",
    )(mom, other)
    groups = [[core + 2 * k for k in range(CHIPS)] for core in range(2)]
    everyone = lax.all_to_all(chip, "gx", 0, 0, axis_index_groups=groups)
    joined = pl.pallas_call(
        join_kernel,
        out_shape=shape(*half),
        in_specs=[VM],
        out_specs=VM,
        compiler_params=params(16),
        name="join",
    )(everyone)
    joined_other = lax.ppermute(joined, "gx", pair_low(nx))
    new = pl.pallas_call(
        final_kernel,
        out_shape=shape(3, X, Y, Z),
        in_specs=[ANY, VM, VM, VM],
        out_specs=ANY,
        scratch_shapes=[pltpu.VMEM((3, X, Y, Z), F32)] * 2 + sems * 2,
        compiler_params=params(16),
        name="final",
    )(u, joined, joined_other, other)
    return new, n


def solution(mesh):
    spec = P(None, "gx", None, "gz")
    return jax.shard_map(shards, mesh=mesh, in_specs=(spec,), out_specs=(spec, spec), check_vma=False)
```

```python
import math

import jax
import jax.numpy as jnp
from jax import lax
from jax.experimental import pallas as pl
from jax.experimental.pallas import tpu as pltpu
from jax.sharding import PartitionSpec as P

VISC = 12288
COURANT = 0.1

HALF = 1.0 / (2.0 * VISC)
LAM = 1.0 + HALF - math.sqrt(2.0 * HALF + HALF * HALF)
GAIN = 1.0 / (1.0 + 2.0 * VISC * (1.0 - LAM))

X = 64
Y = 32
Z = 128
CHUNK = 8
CHUNKS = X // CHUNK
GROUP = 10
LOAD = 16
LOADS = X // LOAD
GROUPS = (X - 4) // GROUP
PAD = 8
WIDE = Y + 2 * PAD
CHIPS = 8
PERIOD = 2 * X * CHIPS
F32 = jnp.float32
BF16 = jnp.bfloat16
VM = pl.BlockSpec(memory_space=pltpu.VMEM)
ANY = pl.BlockSpec(memory_space=pl.ANY)
HBM = pl.BlockSpec(memory_space=pltpu.HBM)


COST = pl.CostEstimate(flops=20_000_000, bytes_accessed=12_000_000, transcendentals=0)


def params(mib):
    return pltpu.CompilerParams(vmem_limit_bytes=mib * 1024 * 1024)


def shape(*dims):
    return jax.ShapeDtypeStruct(dims, F32)


def lanes(rows):
    return lax.broadcasted_iota(jnp.int32, (rows, Z), 1)


def shift(a, amount):
    return pltpu.roll(a, amount % Z, 1)


def split(a):
    high = a.astype(BF16)
    rest = a - high.astype(F32)
    middle = rest.astype(BF16)
    return high, middle, (rest - middle.astype(F32)).astype(BF16)


def band_matrices():
    gap = (lax.broadcasted_iota(jnp.int32, (Z, Z), 0) - lax.broadcasted_iota(jnp.int32, (Z, Z), 1)) & (Z - 1)
    band = jnp.where(gap == 1, 8.0, 0.0) - jnp.where(gap == Z - 1, 8.0, 0.0)
    band = band - jnp.where(gap == 2, 1.0, 0.0) + jnp.where(gap == Z - 2, 1.0, 0.0)
    band = band.astype(BF16)
    return band, jnp.concatenate([band, band], axis=0)


def z_by_matrix(f, bands):
    one, two, three = split(f)
    pair = jnp.concatenate([one, two], axis=1)
    total = jnp.dot(pair, bands[1], preferred_element_type=F32)
    return total + jnp.dot(three, bands[0], preferred_element_type=F32)


def z_by_shift(f):
    return 8.0 * (shift(f, -1) - shift(f, 1)) - (shift(f, -2) - shift(f, 2))


def advection(vp_ref, x, layer, bands):
    f = layer(x)
    gx = 8.0 * (layer(x + 1) - layer(x - 1)) - (layer(x + 2) - layer(x - 2))
    near = vp_ref[:, x, PAD + 1 : PAD + Y + 1] - vp_ref[:, x, PAD - 1 : PAD + Y - 1]
    gy = 8.0 * near - (vp_ref[:, x, PAD + 2 : PAD + Y + 2] - vp_ref[:, x, PAD - 2 : PAD + Y - 2])
    gz = jnp.concatenate([z_by_matrix(f[:2].reshape(2 * Y, Z), bands), z_by_shift(f[2])], axis=0)
    u = f * (1.0 / 12.0)
    return u[0][None] * gx + u[1][None] * gy + u[2][None] * gz.reshape(3, Y, Z)


def interior(vp_ref, part_ref):
    bands = band_matrices()

    def layer(x):
        return vp_ref[:, x, PAD : PAD + Y]

    def group(g, carry):
        for k in range(GROUP):
            x = 2 + g * GROUP + k
            part_ref[:, x] = advection(vp_ref, x, layer, bands)
        return carry

    lax.fori_loop(0, GROUPS, group, 0)


def place():
    return lax.rem(lax.axis_index("gz"), 8)


def pack_kernel(v_ref, zb_ref, za_ref, xb_ref, xa_ref, vp_ref, part_ref, sem):
    def v_copy(j):
        rows = pl.ds(j * LOAD, LOAD)
        return pltpu.make_async_copy(v_ref.at[:, rows], vp_ref.at[:, rows, pl.ds(PAD, Y)], sem.at[j])

    for j in range(LOADS):
        v_copy(j).start()
    slot = lanes(3 * Y) >> 1

    def chunk(j, carry):
        bottom, top = carry
        v_copy(j).wait()
        for k in range(LOAD):
            x = j * LOAD + k
            f = vp_ref[:, x, PAD : PAD + Y]
            vp_ref[:, x, PAD - 2 : PAD] = f[:, Y - 2 :]
            vp_ref[:, x, PAD + Y : PAD + Y + 2] = f[:, :2]
            turned = pltpu.roll(f.reshape(3 * Y, Z), 2 * x, 1)
            bottom = jnp.where(slot == x, turned, bottom)
            top = jnp.where(slot == lax.rem(x + X - 1, X), turned, top)
        return bottom, top

    zero = jnp.zeros((3 * Y, Z), F32)
    bottom, top = lax.fori_loop(0, LOADS, chunk, (zero, zero))
    even = lax.rem(lax.axis_index("gz"), 2) == 0
    za_ref[: 3 * Y] = jnp.where(even, top, bottom)
    zb_ref[: 3 * Y] = jnp.where(even, bottom, top)
    za_ref[3 * Y :] = jnp.zeros((za_ref.shape[0] - 3 * Y, Z), F32)
    zb_ref[3 * Y :] = jnp.zeros((zb_ref.shape[0] - 3 * Y, Z), F32)
    first = (1 - lax.rem(lax.axis_index("gx"), 2)) * (X - 2)
    xa_ref[...] = vp_ref[:, pl.ds(first, 2), PAD : PAD + Y]
    xb_ref[...] = vp_ref[:, pl.ds(X - 2 - first, 2), PAD : PAD + Y]

    @pl.when(place() == 0)
    def _():
        interior(vp_ref, part_ref)


def second_kernel(vp_ref, part_ref, za_ref, out_ref, za_out_ref):
    za_out_ref[...] = za_ref[...]

    @pl.when(place() == 1)
    def _():
        interior(vp_ref, out_ref)


def third_kernel(vp_ref, part_ref, out_ref):
    @pl.when(place() > 1)
    def _():
        interior(vp_ref, out_ref)


def stencil_kernel(
    vp_ref, part_ref, xb_ref, xa_ref, za_ref, zb_ref, rb_ref, ra_ref,
    n_ref, w_ref, r_ref, mom_ref,
    nb, edge, xlow, xhigh, nsem,
):
    x_even = lax.rem(lax.axis_index("gx"), 2) == 0
    z_even = lax.rem(lax.axis_index("gz"), 2) == 0
    xlow[...] = jnp.where(x_even, xb_ref[...], xa_ref[...])
    xhigh[...] = jnp.where(x_even, xa_ref[...], xb_ref[...])

    lane = lanes(3 * Y)
    even_lane = lane & 1 == 0
    columns = slice(0, 3 * Y)
    own_top = jnp.where(z_even, za_ref[columns], zb_ref[columns])
    own_bottom = jnp.where(z_even, zb_ref[columns], za_ref[columns])
    high = jnp.where(z_even, ra_ref[columns], rb_ref[columns]) - own_bottom
    low = jnp.where(z_even, rb_ref[columns], ra_ref[columns]) - own_top
    low_two = shift(low, 2)
    at_bottom = jnp.where(even_lane, low_two - 8.0 * shift(low, 1), low_two)
    high_two = shift(high, -2)
    at_top = jnp.where(even_lane, -high_two, 8.0 * shift(high, -1) - high_two)
    early = lane & 3 < 2
    edge[0] = jnp.where(early, at_bottom, at_top)
    edge[1] = jnp.where(early, at_top, at_bottom)
    border = (lane < 2) | (lane >= Z - 2)

    bands = band_matrices()

    def layer(x):
        if isinstance(x, int) and x < 0:
            return xlow[:, x + 2]
        if isinstance(x, int) and x >= X:
            return xhigh[:, x - X]
        return vp_ref[:, x, PAD : PAD + Y]

    def row(x, odd, p, q, power, part):
        f = layer(x)
        fix = jnp.where(border, pltpu.roll(edge[odd], lax.rem(2 * (X - x), Z), 1), 0.0)
        n = part + (f[2] * (1.0 / 12.0))[None] * fix.reshape(3, Y, Z)
        w = (2.0 * GAIN) * f - (COURANT * GAIN) * n
        p = LAM * p + w
        q = q + power * w
        nb[:, x] = n
        w_ref[:, x] = w
        r_ref[:, x] = p - f
        return p, q

    def n_copy(start, size, k):
        rows = pl.ds(start, size)
        return pltpu.make_async_copy(nb.at[:, rows], n_ref.at[:, rows], nsem.at[k])

    p = jnp.zeros((3, Y, Z), F32)
    q = p
    for x in (0, 1):
        p, q = row(x, x % 2, p, q, LAM**x, advection(vp_ref, x, layer, bands))
    n_copy(0, 2, GROUPS).start()

    def group(g, carry):
        p, q, power = carry
        for k in range(GROUP):
            x = 2 + g * GROUP + k
            p, q = row(x, k % 2, p, q, power, part_ref[:, x])
            power = power * LAM
        n_copy(2 + g * GROUP, GROUP, g).start()
        return p, q, power

    p, q, _ = lax.fori_loop(0, GROUPS, group, (p, q, F32(LAM**2)))
    for x in (X - 2, X - 1):
        p, q = row(x, x % 2, p, q, LAM**x, advection(vp_ref, x, layer, bands))
    n_copy(X - 2, 2, GROUPS + 1).start()
    mom_ref[0] = p
    mom_ref[1] = q
    n_copy(0, 2, GROUPS).wait()
    for g in range(GROUPS):
        n_copy(2 + g * GROUP, GROUP, g).wait()
    n_copy(X - 2, 2, GROUPS + 1).wait()


def chip_kernel(own_ref, other_ref, out_ref):
    core = lax.rem(lax.axis_index("gx"), 2)
    rows = pl.ds(pl.multiple_of(core * (Y // 2), Y // 2), Y // 2)
    own_p, own_q = own_ref[0, :, rows], own_ref[1, :, rows]
    other_p, other_q = other_ref[0, :, rows], other_ref[1, :, rows]
    first = core == 0
    far = LAM**X
    p = jnp.where(first, own_p, other_p) * far + jnp.where(first, other_p, own_p)
    q = jnp.where(first, own_q, other_q) + far * jnp.where(first, other_q, own_q)
    for k in range(CHIPS):
        out_ref[k, 0] = p
        out_ref[k, 1] = q


def join_kernel(all_ref, out_ref):
    chip = lax.div(lax.axis_index("gx"), 2)
    p = jnp.zeros(all_ref.shape[2:], F32)
    q = p
    for s in range(1, CHIPS + 1):
        weight = LAM ** (2 * X * (s - 1)) / (1.0 - LAM**PERIOD)
        p = p + weight * all_ref[lax.rem(chip + CHIPS - s % CHIPS, CHIPS), 0]
        q = q + weight * all_ref[lax.rem(chip + s, CHIPS), 1]
    out_ref[0] = p
    out_ref[1] = q


def final_kernel(w_ref, r_ref, in_own_ref, in_other_ref, other_ref, out_ref, ob, osem):
    def o_copy(j):
        rows = pl.ds(j * CHUNK, CHUNK)
        return pltpu.make_async_copy(ob.at[:, rows], out_ref.at[:, rows], osem.at[j])

    first = lax.rem(lax.axis_index("gx"), 2) == 0
    own, other = in_own_ref[...], in_other_ref[...]
    both = jnp.concatenate([jnp.where(first, own, other), jnp.where(first, other, own)], axis=2)
    far = LAM**X
    p_in = jnp.where(first, both[0], other_ref[0] + far * both[0])
    q_in = jnp.where(first, other_ref[1] + far * both[1], both[1])

    def chunk(i, carry):
        p, q = carry
        j = CHUNKS - 1 - i
        for k in reversed(range(CHUNK)):
            x = j * CHUNK + k
            q = LAM * q
            ob[:, x] = (r_ref[:, x] + p) + q
            q = q + w_ref[:, x]
            p = p * (1.0 / LAM)
        o_copy(j).start()
        return p, q

    lax.fori_loop(0, CHUNKS, chunk, (far * p_in, q_in))
    for j in range(CHUNKS):
        o_copy(j).wait()


def pair_low(count):
    return [(i, i ^ 1) for i in range(count)]


def pair_high(count):
    return [(i, (i + 1 if i % 2 else i - 1) % count) for i in range(count)]


def shards(v):
    nx, nz = lax.axis_size("gx"), lax.axis_size("gz")
    v = pltpu.with_memory_space_constraint(v, pltpu.HBM)
    sems = [pltpu.SemaphoreType.DMA((CHUNKS,))]
    part_shape = pltpu.VMEM((3, X, Y, Z), F32)
    zb, za, xb, xa, vp, part = pl.pallas_call(
        pack_kernel,
        out_shape=[shape(208, Z), shape(200, Z)] + [shape(3, 2, Y, Z)] * 2 + [shape(3, X, WIDE, Z), part_shape],
        in_specs=[HBM],
        out_specs=[VM] * 6,
        scratch_shapes=[pltpu.SemaphoreType.DMA((LOADS,))],
        compiler_params=params(16),
        name="pack",
    )(v)
    rzb = lax.ppermute(zb, "gz", pair_high(nz))
    part, za = pl.pallas_call(
        second_kernel,
        out_shape=[part_shape, shape(200, Z)],
        in_specs=[VM] * 3,
        out_specs=[VM] * 2,
        input_output_aliases={1: 0},
        compiler_params=params(16),
        cost_estimate=COST,
        name="second",
    )(vp, part, za)
    rza = lax.ppermute(za, "gz", pair_low(nz))
    rxb = lax.ppermute(xb, "gx", pair_high(nx))
    rxa = lax.ppermute(xa, "gx", pair_low(nx))
    part = pl.pallas_call(
        third_kernel,
        out_shape=part_shape,
        in_specs=[VM] * 2,
        out_specs=VM,
        input_output_aliases={1: 0},
        compiler_params=params(16),
        cost_estimate=COST,
        name="third",
    )(vp, part)
    n, w, r, mom = pl.pallas_call(
        stencil_kernel,
        out_shape=[shape(3, X, Y, Z)] * 3 + [shape(2, 3, Y, Z)],
        in_specs=[VM] * 8,
        out_specs=[ANY, VM, VM, VM],
        scratch_shapes=[
            pltpu.VMEM((3, X, Y, Z), F32),
            pltpu.VMEM((2, 3 * Y, Z), F32),
            pltpu.VMEM((3, 2, Y, Z), F32),
            pltpu.VMEM((3, 2, Y, Z), F32),
            pltpu.SemaphoreType.DMA((GROUPS + 2,)),
        ],
        compiler_params=params(24),
        name="stencil",
    )(vp, part, rxb, rxa, za, zb, rzb, rza)
    other = lax.ppermute(mom, "gx", pair_low(nx))
    half = (2, 3, Y // 2, Z)
    chip = pl.pallas_call(
        chip_kernel,
        out_shape=shape(CHIPS, *half),
        in_specs=[VM, VM],
        out_specs=VM,
        compiler_params=params(16),
        name="chip",
    )(mom, other)
    groups = [[core + 2 * k for k in range(CHIPS)] for core in range(2)]
    everyone = lax.all_to_all(chip, "gx", 0, 0, axis_index_groups=groups)
    joined = pl.pallas_call(
        join_kernel,
        out_shape=shape(*half),
        in_specs=[VM],
        out_specs=VM,
        compiler_params=params(16),
        name="join",
    )(everyone)
    joined_other = lax.ppermute(joined, "gx", pair_low(nx))
    new = pl.pallas_call(
        final_kernel,
        out_shape=shape(3, X, Y, Z),
        in_specs=[VM] * 5,
        out_specs=ANY,
        scratch_shapes=[pltpu.VMEM((3, X, Y, Z), F32)] + sems,
        compiler_params=params(16),
        name="final",
    )(w, r, joined, joined_other, other)
    return new, n


def solution(mesh):
    spec = P(None, "gx", None, "gz")
    return jax.shard_map(shards, mesh=mesh, in_specs=(spec,), out_specs=(spec, spec), check_vma=False)
```

```python
import math

import jax
import jax.numpy as jnp
from jax import lax
from jax.experimental import pallas as pl
from jax.experimental.pallas import tpu as pltpu
from jax.sharding import PartitionSpec as P

VISC = 12288
COURANT = 0.1

HALF = 1.0 / (2.0 * VISC)
LAM = 1.0 + HALF - math.sqrt(2.0 * HALF + HALF * HALF)
GAIN = 1.0 / (1.0 + 2.0 * VISC * (1.0 - LAM))

X = 64
Y = 32
Z = 128
CHUNK = 8
CHUNKS = X // CHUNK
GROUP = 10
LOAD = 16
LOADS = X // LOAD
GROUPS = (X - 4) // GROUP
PAD = 8
WIDE = Y + 2 * PAD
CHIPS = 8
PERIOD = 2 * X * CHIPS
F32 = jnp.float32
BF16 = jnp.bfloat16
VM = pl.BlockSpec(memory_space=pltpu.VMEM)
ANY = pl.BlockSpec(memory_space=pl.ANY)
HBM = pl.BlockSpec(memory_space=pltpu.HBM)


COST = pl.CostEstimate(flops=20_000_000, bytes_accessed=12_000_000, transcendentals=0)


def params(mib):
    return pltpu.CompilerParams(vmem_limit_bytes=mib * 1024 * 1024)


def shape(*dims):
    return jax.ShapeDtypeStruct(dims, F32)


def lanes(rows):
    return lax.broadcasted_iota(jnp.int32, (rows, Z), 1)


def shift(a, amount):
    return pltpu.roll(a, amount % Z, 1)


def split(a):
    high = a.astype(BF16)
    rest = a - high.astype(F32)
    middle = rest.astype(BF16)
    return high, middle, (rest - middle.astype(F32)).astype(BF16)


def band_matrices():
    gap = (lax.broadcasted_iota(jnp.int32, (Z, Z), 0) - lax.broadcasted_iota(jnp.int32, (Z, Z), 1)) & (Z - 1)
    band = jnp.where(gap == 1, 8.0, 0.0) - jnp.where(gap == Z - 1, 8.0, 0.0)
    band = band - jnp.where(gap == 2, 1.0, 0.0) + jnp.where(gap == Z - 2, 1.0, 0.0)
    band = band.astype(BF16)
    return band, jnp.concatenate([band, band], axis=0)


def z_by_matrix(f, bands):
    one, two, three = split(f)
    pair = jnp.concatenate([one, two], axis=1)
    total = jnp.dot(pair, bands[1], preferred_element_type=F32)
    return total + jnp.dot(three, bands[0], preferred_element_type=F32)


def z_by_shift(f):
    return 8.0 * (shift(f, -1) - shift(f, 1)) - (shift(f, -2) - shift(f, 2))


def advection(vp_ref, x, layer, bands):
    f = layer(x)
    gx = 8.0 * (layer(x + 1) - layer(x - 1)) - (layer(x + 2) - layer(x - 2))
    near = vp_ref[:, x, PAD + 1 : PAD + Y + 1] - vp_ref[:, x, PAD - 1 : PAD + Y - 1]
    gy = 8.0 * near - (vp_ref[:, x, PAD + 2 : PAD + Y + 2] - vp_ref[:, x, PAD - 2 : PAD + Y - 2])
    gz = jnp.concatenate([z_by_matrix(f[:2].reshape(2 * Y, Z), bands), z_by_shift(f[2])], axis=0)
    u = f * (1.0 / 12.0)
    return u[0][None] * gx + u[1][None] * gy + u[2][None] * gz.reshape(3, Y, Z)


def interior(vp_ref, part_ref):
    bands = band_matrices()

    def layer(x):
        return vp_ref[:, x, PAD : PAD + Y]

    def group(g, carry):
        for k in range(GROUP):
            x = 2 + g * GROUP + k
            part_ref[:, x] = advection(vp_ref, x, layer, bands)
        return carry

    lax.fori_loop(0, GROUPS, group, 0)


def place():
    return lax.rem(lax.axis_index("gz"), 8)


def pack_kernel(v_ref, zb_ref, za_ref, xb_ref, xa_ref, vp_ref, part_ref, sem):
    def v_copy(j):
        rows = pl.ds(j * LOAD, LOAD)
        return pltpu.make_async_copy(v_ref.at[:, rows], vp_ref.at[:, rows, pl.ds(PAD, Y)], sem.at[j])

    for j in range(LOADS):
        v_copy(j).start()
    slot = lanes(3 * Y) >> 1

    def chunk(j, carry):
        bottom, top = carry
        v_copy(j).wait()
        for k in range(LOAD):
            x = j * LOAD + k
            f = vp_ref[:, x, PAD : PAD + Y]
            vp_ref[:, x, PAD - 2 : PAD] = f[:, Y - 2 :]
            vp_ref[:, x, PAD + Y : PAD + Y + 2] = f[:, :2]
            turned = pltpu.roll(f.reshape(3 * Y, Z), 2 * x, 1)
            bottom = jnp.where(slot == x, turned, bottom)
            top = jnp.where(slot == lax.rem(x + X - 1, X), turned, top)
        return bottom, top

    zero = jnp.zeros((3 * Y, Z), F32)
    bottom, top = lax.fori_loop(0, LOADS, chunk, (zero, zero))
    even = lax.rem(lax.axis_index("gz"), 2) == 0
    za_ref[: 3 * Y] = jnp.where(even, top, bottom)
    zb_ref[: 3 * Y] = jnp.where(even, bottom, top)
    za_ref[3 * Y :] = jnp.zeros((za_ref.shape[0] - 3 * Y, Z), F32)
    zb_ref[3 * Y :] = jnp.zeros((zb_ref.shape[0] - 3 * Y, Z), F32)
    first = (1 - lax.rem(lax.axis_index("gx"), 2)) * (X - 2)
    xa_ref[...] = vp_ref[:, pl.ds(first, 2), PAD : PAD + Y]
    xb_ref[...] = vp_ref[:, pl.ds(X - 2 - first, 2), PAD : PAD + Y]

    @pl.when(place() == 0)
    def _():
        interior(vp_ref, part_ref)


def second_kernel(vp_ref, part_ref, za_ref, out_ref, za_out_ref):
    za_out_ref[...] = za_ref[...]

    @pl.when(place() == 1)
    def _():
        interior(vp_ref, out_ref)


def third_kernel(vp_ref, part_ref, out_ref):
    @pl.when(place() > 1)
    def _():
        interior(vp_ref, out_ref)


def border_term(edge, x, u_z):
    lane = lanes(3 * Y)
    border = (lane < 2) | (lane >= Z - 2)
    fix = jnp.where(border, pltpu.roll(edge, lax.rem(2 * (X - x), Z), 1), 0.0)
    return u_z[None] * fix.reshape(3, Y, Z)


def source(f, n):
    return (2.0 * GAIN) * f - (COURANT * GAIN) * n


def stencil_kernel(
    vp_ref, part_ref, za_ref, zb_ref, rb_ref, ra_ref,
    n_ref, w_ref, r_ref, sum_ref, edge_ref,
):
    z_even = lax.rem(lax.axis_index("gz"), 2) == 0
    lane = lanes(3 * Y)
    even_lane = lane & 1 == 0
    columns = slice(0, 3 * Y)
    own_top = jnp.where(z_even, za_ref[columns], zb_ref[columns])
    own_bottom = jnp.where(z_even, zb_ref[columns], za_ref[columns])
    high = jnp.where(z_even, ra_ref[columns], rb_ref[columns]) - own_bottom
    low = jnp.where(z_even, rb_ref[columns], ra_ref[columns]) - own_top
    low_two = shift(low, 2)
    at_bottom = jnp.where(even_lane, low_two - 8.0 * shift(low, 1), low_two)
    high_two = shift(high, -2)
    at_top = jnp.where(even_lane, -high_two, 8.0 * shift(high, -1) - high_two)
    early = lane & 3 < 2
    edge_ref[0] = jnp.where(early, at_bottom, at_top)
    edge_ref[1] = jnp.where(early, at_top, at_bottom)

    def group(g, carry):
        p, q, power = carry
        for k in range(GROUP):
            x = 2 + g * GROUP + k
            f = vp_ref[:, x, PAD : PAD + Y]
            n = part_ref[:, x] + border_term(edge_ref[k % 2], x, f[2] * (1.0 / 12.0))
            w = source(f, n)
            p = LAM * p + w
            q = q + power * w
            n_ref[:, x] = n
            w_ref[:, x] = w
            r_ref[:, x] = p - f
            power = power * LAM
        return p, q, power

    zero = jnp.zeros((3, Y, Z), F32)
    sum_ref[0], sum_ref[1], _ = lax.fori_loop(0, GROUPS, group, (zero, zero, F32(1.0)))


def ends_kernel(
    vp_ref, edge_ref, sum_ref, xb_ref, xa_ref,
    n_ref, w_ref, r_ref, start_ref, mom_ref,
):
    x_even = lax.rem(lax.axis_index("gx"), 2) == 0
    xlow = jnp.where(x_even, xb_ref[...], xa_ref[...])
    xhigh = jnp.where(x_even, xa_ref[...], xb_ref[...])
    bands = band_matrices()

    def layer(x):
        if x < 0:
            return xlow[:, x + 2]
        if x >= X:
            return xhigh[:, x - X]
        return vp_ref[:, x, PAD : PAD + Y]

    fields, sources = [], []
    for k, x in enumerate((0, 1, X - 2, X - 1)):
        f = layer(x)
        n = advection(vp_ref, x, layer, bands) + border_term(edge_ref[x % 2], x, f[2] * (1.0 / 12.0))
        w = source(f, n)
        n_ref[:, k] = n
        w_ref[:, k] = w
        fields.append(f)
        sources.append(w)
    start = LAM * sources[0] + sources[1]
    before_last = LAM * (sum_ref[0] + LAM ** (X - 4) * start) + sources[2]
    last = LAM * before_last + sources[3]
    for k, p in enumerate((sources[0], start, before_last, last)):
        r_ref[:, k] = p - fields[k]
    start_ref[...] = start
    mom_ref[0] = last
    ends = LAM ** (X - 2) * sources[2] + LAM ** (X - 1) * sources[3]
    mom_ref[1] = sources[0] + LAM * sources[1] + LAM**2 * sum_ref[1] + ends


def store_first_kernel(n_ref, ends_ref, out_ref, sems):
    copies = [
        pltpu.make_async_copy(n_ref.at[:, 2 : X // 2], out_ref.at[:, 2 : X // 2], sems.at[0]),
        pltpu.make_async_copy(ends_ref.at[:, 0:2], out_ref.at[:, 0:2], sems.at[1]),
    ]
    for copy in copies:
        copy.start()
    for copy in copies:
        copy.wait()


def store_last_kernel(n_ref, ends_ref, started_ref, out_ref, sems):
    copies = [
        pltpu.make_async_copy(n_ref.at[:, X // 2 : X - 2], out_ref.at[:, X // 2 : X - 2], sems.at[0]),
        pltpu.make_async_copy(ends_ref.at[:, 2:4], out_ref.at[:, X - 2 : X], sems.at[1]),
    ]
    for copy in copies:
        copy.start()
    for copy in copies:
        copy.wait()


def chip_kernel(own_ref, other_ref, started_ref, out_ref):
    core = lax.rem(lax.axis_index("gx"), 2)
    rows = pl.ds(pl.multiple_of(core * (Y // 2), Y // 2), Y // 2)
    own_p, own_q = own_ref[0, :, rows], own_ref[1, :, rows]
    other_p, other_q = other_ref[0, :, rows], other_ref[1, :, rows]
    first = core == 0
    far = LAM**X
    p = jnp.where(first, own_p, other_p) * far + jnp.where(first, other_p, own_p)
    q = jnp.where(first, own_q, other_q) + far * jnp.where(first, other_q, own_q)
    for k in range(CHIPS):
        out_ref[k, 0] = p
        out_ref[k, 1] = q


def join_kernel(all_ref, out_ref):
    chip = lax.div(lax.axis_index("gx"), 2)
    p = jnp.zeros(all_ref.shape[2:], F32)
    q = p
    for s in range(1, CHIPS + 1):
        weight = LAM ** (2 * X * (s - 1)) / (1.0 - LAM**PERIOD)
        p = p + weight * all_ref[lax.rem(chip + CHIPS - s % CHIPS, CHIPS), 0]
        q = q + weight * all_ref[lax.rem(chip + s, CHIPS), 1]
    out_ref[0] = p
    out_ref[1] = q


def final_kernel(
    w_ref, r_ref, wend_ref, rend_ref, start_ref, in_own_ref, in_other_ref, other_ref, out_ref, ob, osem,
):
    def o_copy(start, size, k):
        rows = pl.ds(start, size)
        return pltpu.make_async_copy(ob.at[:, rows], out_ref.at[:, rows], osem.at[k])

    first = lax.rem(lax.axis_index("gx"), 2) == 0
    own, other = in_own_ref[...], in_other_ref[...]
    both = jnp.concatenate([jnp.where(first, own, other), jnp.where(first, other, own)], axis=2)
    far = LAM**X
    p_in = jnp.where(first, both[0], other_ref[0] + far * both[0])
    q = jnp.where(first, other_ref[1] + far * both[1], both[1])

    for k, x in ((3, X - 1), (2, X - 2)):
        q = LAM * q
        ob[:, x] = (rend_ref[:, k] + LAM ** (x + 1) * p_in) + q
        q = q + wend_ref[:, k]
    o_copy(X - 2, 2, GROUPS).start()

    def group(i, carry):
        p, q = carry
        g = GROUPS - 1 - i
        for k in reversed(range(GROUP)):
            x = 2 + g * GROUP + k
            q = LAM * q
            ob[:, x] = (r_ref[:, x] + p) + q
            q = q + w_ref[:, x]
            p = p * (1.0 / LAM)
        o_copy(2 + g * GROUP, GROUP, g).start()
        return p, q

    p = LAM ** (X - 2) * p_in + LAM ** (X - 4) * start_ref[...]
    _, q = lax.fori_loop(0, GROUPS, group, (p, q))
    for x in (1, 0):
        q = LAM * q
        ob[:, x] = (rend_ref[:, x] + LAM ** (x + 1) * p_in) + q
        q = q + wend_ref[:, x]
    o_copy(0, 2, GROUPS + 1).start()
    o_copy(X - 2, 2, GROUPS).wait()
    for g in range(GROUPS):
        o_copy(2 + g * GROUP, GROUP, g).wait()
    o_copy(0, 2, GROUPS + 1).wait()


def pair_low(count):
    return [(i, i ^ 1) for i in range(count)]


def pair_high(count):
    return [(i, (i + 1 if i % 2 else i - 1) % count) for i in range(count)]


def shards(v):
    nx, nz = lax.axis_size("gx"), lax.axis_size("gz")
    v = pltpu.with_memory_space_constraint(v, pltpu.HBM)
    sems = [pltpu.SemaphoreType.DMA((CHUNKS,))]
    part_shape = pltpu.VMEM((3, X, Y, Z), F32)
    zb, za, xb, xa, vp, part = pl.pallas_call(
        pack_kernel,
        out_shape=[shape(208, Z), shape(200, Z)] + [shape(3, 2, Y, Z)] * 2 + [shape(3, X, WIDE, Z), part_shape],
        in_specs=[HBM],
        out_specs=[VM] * 6,
        scratch_shapes=[pltpu.SemaphoreType.DMA((LOADS,))],
        compiler_params=params(16),
        name="pack",
    )(v)
    rzb = lax.ppermute(zb, "gz", pair_high(nz))
    part, za = pl.pallas_call(
        second_kernel,
        out_shape=[part_shape, shape(200, Z)],
        in_specs=[VM] * 3,
        out_specs=[VM] * 2,
        input_output_aliases={1: 0},
        compiler_params=params(16),
        cost_estimate=COST,
        name="second",
    )(vp, part, za)
    rza = lax.ppermute(za, "gz", pair_low(nz))
    rxb = lax.ppermute(xb, "gx", pair_high(nx))
    rxa = lax.ppermute(xa, "gx", pair_low(nx))
    part = pl.pallas_call(
        third_kernel,
        out_shape=part_shape,
        in_specs=[VM] * 2,
        out_specs=VM,
        input_output_aliases={1: 0},
        compiler_params=params(16),
        cost_estimate=COST,
        name="third",
    )(vp, part)
    n, w, r, sums, edge = pl.pallas_call(
        stencil_kernel,
        out_shape=[part_shape] * 3 + [shape(2, 3, Y, Z), shape(2, 3 * Y, Z)],
        in_specs=[VM] * 6,
        out_specs=[VM] * 5,
        compiler_params=params(16),
        cost_estimate=COST,
        name="stencil",
    )(vp, part, za, zb, rzb, rza)
    n_ends, w_ends, r_ends, start, mom = pl.pallas_call(
        ends_kernel,
        out_shape=[shape(3, 4, Y, Z)] * 3 + [shape(3, Y, Z), shape(2, 3, Y, Z)],
        in_specs=[VM] * 5,
        out_specs=[VM] * 5,
        compiler_params=params(16),
        name="ends",
    )(vp, edge, sums, rxb, rxa)
    other = lax.ppermute(mom, "gx", pair_low(nx))
    half_cost = pl.CostEstimate(flops=0, bytes_accessed=4_000_000, transcendentals=0)
    stored = pl.pallas_call(
        store_first_kernel,
        out_shape=shape(3, X, Y, Z),
        in_specs=[VM] * 2,
        out_specs=HBM,
        scratch_shapes=[pltpu.SemaphoreType.DMA((2,))],
        compiler_params=params(8),
        cost_estimate=half_cost,
        name="store_first",
    )(n, n_ends)
    stored = pltpu.with_memory_space_constraint(stored, pltpu.HBM)
    half = (2, 3, Y // 2, Z)
    chip = pl.pallas_call(
        chip_kernel,
        out_shape=shape(CHIPS, *half),
        in_specs=[VM, VM, HBM],
        out_specs=VM,
        compiler_params=params(16),
        name="chip",
    )(mom, other, stored)
    groups = [[core + 2 * k for k in range(CHIPS)] for core in range(2)]
    everyone = lax.all_to_all(chip, "gx", 0, 0, axis_index_groups=groups)
    joined = pl.pallas_call(
        join_kernel,
        out_shape=shape(*half),
        in_specs=[VM],
        out_specs=VM,
        compiler_params=params(16),
        name="join",
    )(everyone)
    joined_other = lax.ppermute(joined, "gx", pair_low(nx))
    stored = pl.pallas_call(
        store_last_kernel,
        out_shape=shape(3, X, Y, Z),
        in_specs=[VM, VM, HBM],
        out_specs=HBM,
        input_output_aliases={2: 0},
        scratch_shapes=[pltpu.SemaphoreType.DMA((2,))],
        compiler_params=params(8),
        cost_estimate=half_cost,
        name="store_last",
    )(n, n_ends, stored)
    new = pl.pallas_call(
        final_kernel,
        out_shape=shape(3, X, Y, Z),
        in_specs=[VM] * 8,
        out_specs=ANY,
        scratch_shapes=[pltpu.VMEM((3, X, Y, Z), F32), pltpu.SemaphoreType.DMA((GROUPS + 2,))],
        compiler_params=params(16),
        name="final",
    )(w, r, w_ends, r_ends, start, joined, joined_other, other)
    return new, stored


def solution(mesh):
    spec = P(None, "gx", None, "gz")
    return jax.shard_map(shards, mesh=mesh, in_specs=(spec,), out_specs=(spec, spec), check_vma=False)
```

```python
import math

import jax
import jax.numpy as jnp
from jax import lax
from jax.experimental import pallas as pl
from jax.experimental.pallas import tpu as pltpu
from jax.sharding import PartitionSpec as P

VISC = 12288
COURANT = 0.1

HALF = 1.0 / (2.0 * VISC)
LAM = 1.0 + HALF - math.sqrt(2.0 * HALF + HALF * HALF)
GAIN = 1.0 / (1.0 + 2.0 * VISC * (1.0 - LAM))

X = 64
Y = 32
Z = 128
CHUNK = 8
CHUNKS = X // CHUNK
GROUP = 10
LOAD = 16
LOADS = X // LOAD
GROUPS = (X - 4) // GROUP
FIRST = 2 + 2 * GROUP
SECOND = 2 + 4 * GROUP
PAD = 8
WIDE = Y + 2 * PAD
CHIPS = 8
PERIOD = 2 * X * CHIPS
F32 = jnp.float32
BF16 = jnp.bfloat16
VM = pl.BlockSpec(memory_space=pltpu.VMEM)
ANY = pl.BlockSpec(memory_space=pl.ANY)
HBM = pl.BlockSpec(memory_space=pltpu.HBM)


COST = pl.CostEstimate(flops=20_000_000, bytes_accessed=12_000_000, transcendentals=0)


def params(mib):
    return pltpu.CompilerParams(vmem_limit_bytes=mib * 1024 * 1024)


def shape(*dims):
    return jax.ShapeDtypeStruct(dims, F32)


def lanes(rows):
    return lax.broadcasted_iota(jnp.int32, (rows, Z), 1)


def shift(a, amount):
    return pltpu.roll(a, amount % Z, 1)


def split(a):
    high = a.astype(BF16)
    rest = a - high.astype(F32)
    middle = rest.astype(BF16)
    return high, middle, (rest - middle.astype(F32)).astype(BF16)


def band_matrices():
    gap = (lax.broadcasted_iota(jnp.int32, (Z, Z), 0) - lax.broadcasted_iota(jnp.int32, (Z, Z), 1)) & (Z - 1)
    band = jnp.where(gap == 1, 8.0, 0.0) - jnp.where(gap == Z - 1, 8.0, 0.0)
    band = band - jnp.where(gap == 2, 1.0, 0.0) + jnp.where(gap == Z - 2, 1.0, 0.0)
    band = band.astype(BF16)
    return band, jnp.concatenate([band, band], axis=0)


def z_by_matrix(f, bands):
    one, two, three = split(f)
    pair = jnp.concatenate([one, two], axis=1)
    total = jnp.dot(pair, bands[1], preferred_element_type=F32)
    return total + jnp.dot(three, bands[0], preferred_element_type=F32)


def z_by_shift(f):
    return 8.0 * (shift(f, -1) - shift(f, 1)) - (shift(f, -2) - shift(f, 2))


def advection(vp_ref, x, layer, bands):
    f = layer(x)
    gx = 8.0 * (layer(x + 1) - layer(x - 1)) - (layer(x + 2) - layer(x - 2))
    near = vp_ref[:, x, PAD + 1 : PAD + Y + 1] - vp_ref[:, x, PAD - 1 : PAD + Y - 1]
    gy = 8.0 * near - (vp_ref[:, x, PAD + 2 : PAD + Y + 2] - vp_ref[:, x, PAD - 2 : PAD + Y - 2])
    gz = jnp.concatenate([z_by_matrix(f[:2].reshape(2 * Y, Z), bands), z_by_shift(f[2])], axis=0)
    u = f * (1.0 / 12.0)
    return u[0][None] * gx + u[1][None] * gy + u[2][None] * gz.reshape(3, Y, Z)


def interior(vp_ref, part_ref):
    bands = band_matrices()

    def layer(x):
        return vp_ref[:, x, PAD : PAD + Y]

    def group(g, carry):
        for k in range(GROUP):
            x = 2 + g * GROUP + k
            part_ref[:, x] = advection(vp_ref, x, layer, bands)
        return carry

    lax.fori_loop(0, GROUPS, group, 0)


def place():
    return lax.rem(lax.axis_index("gz"), 8)


def pack_kernel(v_ref, zb_ref, za_ref, xb_ref, xa_ref, vp_ref, part_ref, sem):
    def v_copy(j):
        rows = pl.ds(j * LOAD, LOAD)
        return pltpu.make_async_copy(v_ref.at[:, rows], vp_ref.at[:, rows, pl.ds(PAD, Y)], sem.at[j])

    for j in range(LOADS):
        v_copy(j).start()
    slot = lanes(3 * Y) >> 1

    def chunk(j, carry):
        bottom, top = carry
        v_copy(j).wait()
        for k in range(LOAD):
            x = j * LOAD + k
            f = vp_ref[:, x, PAD : PAD + Y]
            vp_ref[:, x, PAD - 2 : PAD] = f[:, Y - 2 :]
            vp_ref[:, x, PAD + Y : PAD + Y + 2] = f[:, :2]
            turned = pltpu.roll(f.reshape(3 * Y, Z), 2 * x, 1)
            bottom = jnp.where(slot == x, turned, bottom)
            top = jnp.where(slot == lax.rem(x + X - 1, X), turned, top)
        return bottom, top

    zero = jnp.zeros((3 * Y, Z), F32)
    bottom, top = lax.fori_loop(0, LOADS, chunk, (zero, zero))
    even = lax.rem(lax.axis_index("gz"), 2) == 0
    za_ref[: 3 * Y] = jnp.where(even, top, bottom)
    zb_ref[: 3 * Y] = jnp.where(even, bottom, top)
    za_ref[3 * Y :] = jnp.zeros((za_ref.shape[0] - 3 * Y, Z), F32)
    zb_ref[3 * Y :] = jnp.zeros((zb_ref.shape[0] - 3 * Y, Z), F32)
    first = (1 - lax.rem(lax.axis_index("gx"), 2)) * (X - 2)
    xa_ref[...] = vp_ref[:, pl.ds(first, 2), PAD : PAD + Y]
    xb_ref[...] = vp_ref[:, pl.ds(X - 2 - first, 2), PAD : PAD + Y]

    @pl.when(place() == 0)
    def _():
        interior(vp_ref, part_ref)


def second_kernel(vp_ref, part_ref, za_ref, out_ref, za_out_ref):
    za_out_ref[...] = za_ref[...]

    @pl.when(place() == 1)
    def _():
        interior(vp_ref, out_ref)


def third_kernel(vp_ref, part_ref, out_ref):
    @pl.when(place() > 1)
    def _():
        interior(vp_ref, out_ref)


def border_term(edge, x, u_z):
    lane = lanes(3 * Y)
    border = (lane < 2) | (lane >= Z - 2)
    fix = jnp.where(border, pltpu.roll(edge, lax.rem(2 * (X - x), Z), 1), 0.0)
    return u_z[None] * fix.reshape(3, Y, Z)


def source(f, n):
    return (2.0 * GAIN) * f - (COURANT * GAIN) * n


def stencil_kernel(
    vp_ref, part_ref, za_ref, zb_ref, rb_ref, ra_ref,
    n_ref, w_ref, r_ref, sum_ref, edge_ref, stored_ref, sem,
):
    z_even = lax.rem(lax.axis_index("gz"), 2) == 0
    lane = lanes(3 * Y)
    even_lane = lane & 1 == 0
    columns = slice(0, 3 * Y)
    own_top = jnp.where(z_even, za_ref[columns], zb_ref[columns])
    own_bottom = jnp.where(z_even, zb_ref[columns], za_ref[columns])
    high = jnp.where(z_even, ra_ref[columns], rb_ref[columns]) - own_bottom
    low = jnp.where(z_even, rb_ref[columns], ra_ref[columns]) - own_top
    low_two = shift(low, 2)
    at_bottom = jnp.where(even_lane, low_two - 8.0 * shift(low, 1), low_two)
    high_two = shift(high, -2)
    at_top = jnp.where(even_lane, -high_two, 8.0 * shift(high, -1) - high_two)
    early = lane & 3 < 2
    edge_ref[0] = jnp.where(early, at_bottom, at_top)
    edge_ref[1] = jnp.where(early, at_top, at_bottom)

    def group(g, carry):
        p, q, power = carry
        for k in range(GROUP):
            x = 2 + g * GROUP + k
            f = vp_ref[:, x, PAD : PAD + Y]
            n = part_ref[:, x] + border_term(edge_ref[k % 2], x, f[2] * (1.0 / 12.0))
            w = source(f, n)
            p = LAM * p + w
            q = q + power * w
            n_ref[:, x] = n
            w_ref[:, x] = w
            r_ref[:, x] = p - f
            power = power * LAM

        @pl.when(g == 1)
        def _():
            store.start()

        return p, q, power

    store = pltpu.make_async_copy(n_ref.at[:, 2:FIRST], stored_ref.at[:, 2:FIRST], sem)
    zero = jnp.zeros((3, Y, Z), F32)
    sum_ref[0], sum_ref[1], _ = lax.fori_loop(0, GROUPS, group, (zero, zero, F32(1.0)))
    store.wait()


def ends_kernel(
    vp_ref, edge_ref, sum_ref, xb_ref, xa_ref,
    n_ref, w_ref, r_ref, start_ref, mom_ref,
):
    x_even = lax.rem(lax.axis_index("gx"), 2) == 0
    xlow = jnp.where(x_even, xb_ref[...], xa_ref[...])
    xhigh = jnp.where(x_even, xa_ref[...], xb_ref[...])
    bands = band_matrices()

    def layer(x):
        if x < 0:
            return xlow[:, x + 2]
        if x >= X:
            return xhigh[:, x - X]
        return vp_ref[:, x, PAD : PAD + Y]

    fields, sources = [], []
    for k, x in enumerate((0, 1, X - 2, X - 1)):
        f = layer(x)
        n = advection(vp_ref, x, layer, bands) + border_term(edge_ref[x % 2], x, f[2] * (1.0 / 12.0))
        w = source(f, n)
        n_ref[:, k] = n
        w_ref[:, k] = w
        fields.append(f)
        sources.append(w)
    start = LAM * sources[0] + sources[1]
    before_last = LAM * (sum_ref[0] + LAM ** (X - 4) * start) + sources[2]
    last = LAM * before_last + sources[3]
    for k, p in enumerate((sources[0], start, before_last, last)):
        r_ref[:, k] = p - fields[k]
    start_ref[...] = start
    mom_ref[0] = last
    ends = LAM ** (X - 2) * sources[2] + LAM ** (X - 1) * sources[3]
    mom_ref[1] = sources[0] + LAM * sources[1] + LAM**2 * sum_ref[1] + ends


def store_first_kernel(n_ref, ends_ref, started_ref, out_ref, sems):
    copies = [
        pltpu.make_async_copy(n_ref.at[:, FIRST:SECOND], out_ref.at[:, FIRST:SECOND], sems.at[0]),
        pltpu.make_async_copy(ends_ref.at[:, 0:2], out_ref.at[:, 0:2], sems.at[1]),
    ]
    for copy in copies:
        copy.start()
    for copy in copies:
        copy.wait()


def store_last_kernel(n_ref, ends_ref, started_ref, out_ref, sems):
    copies = [
        pltpu.make_async_copy(n_ref.at[:, SECOND : X - 2], out_ref.at[:, SECOND : X - 2], sems.at[0]),
        pltpu.make_async_copy(ends_ref.at[:, 2:4], out_ref.at[:, X - 2 : X], sems.at[1]),
    ]
    for copy in copies:
        copy.start()
    for copy in copies:
        copy.wait()


def chip_kernel(own_ref, other_ref, started_ref, out_ref):
    core = lax.rem(lax.axis_index("gx"), 2)
    rows = pl.ds(pl.multiple_of(core * (Y // 2), Y // 2), Y // 2)
    own_p, own_q = own_ref[0, :, rows], own_ref[1, :, rows]
    other_p, other_q = other_ref[0, :, rows], other_ref[1, :, rows]
    first = core == 0
    far = LAM**X
    p = jnp.where(first, own_p, other_p) * far + jnp.where(first, other_p, own_p)
    q = jnp.where(first, own_q, other_q) + far * jnp.where(first, other_q, own_q)
    for k in range(CHIPS):
        out_ref[k, 0] = p
        out_ref[k, 1] = q


def join_kernel(all_ref, out_ref):
    chip = lax.div(lax.axis_index("gx"), 2)
    p = jnp.zeros(all_ref.shape[2:], F32)
    q = p
    for s in range(1, CHIPS + 1):
        weight = LAM ** (2 * X * (s - 1)) / (1.0 - LAM**PERIOD)
        p = p + weight * all_ref[lax.rem(chip + CHIPS - s % CHIPS, CHIPS), 0]
        q = q + weight * all_ref[lax.rem(chip + s, CHIPS), 1]
    out_ref[0] = p
    out_ref[1] = q


def final_kernel(
    w_ref, r_ref, wend_ref, rend_ref, start_ref, in_own_ref, in_other_ref, other_ref, out_ref, ob, osem,
):
    def o_copy(start, size, k):
        rows = pl.ds(start, size)
        return pltpu.make_async_copy(ob.at[:, rows], out_ref.at[:, rows], osem.at[k])

    first = lax.rem(lax.axis_index("gx"), 2) == 0
    own, other = in_own_ref[...], in_other_ref[...]
    both = jnp.concatenate([jnp.where(first, own, other), jnp.where(first, other, own)], axis=2)
    far = LAM**X
    p_in = jnp.where(first, both[0], other_ref[0] + far * both[0])
    q = jnp.where(first, other_ref[1] + far * both[1], both[1])

    for k, x in ((3, X - 1), (2, X - 2)):
        q = LAM * q
        ob[:, x] = (rend_ref[:, k] + LAM ** (x + 1) * p_in) + q
        q = q + wend_ref[:, k]
    o_copy(X - 2, 2, GROUPS).start()

    def group(i, carry):
        p, q = carry
        g = GROUPS - 1 - i
        for k in reversed(range(GROUP)):
            x = 2 + g * GROUP + k
            q = LAM * q
            ob[:, x] = (r_ref[:, x] + p) + q
            q = q + w_ref[:, x]
            p = p * (1.0 / LAM)
        o_copy(2 + g * GROUP, GROUP, g).start()
        return p, q

    p = LAM ** (X - 2) * p_in + LAM ** (X - 4) * start_ref[...]
    _, q = lax.fori_loop(0, GROUPS, group, (p, q))
    for x in (1, 0):
        q = LAM * q
        ob[:, x] = (rend_ref[:, x] + LAM ** (x + 1) * p_in) + q
        q = q + wend_ref[:, x]
    o_copy(0, 2, GROUPS + 1).start()
    o_copy(X - 2, 2, GROUPS).wait()
    for g in range(GROUPS):
        o_copy(2 + g * GROUP, GROUP, g).wait()
    o_copy(0, 2, GROUPS + 1).wait()


def pair_low(count):
    return [(i, i ^ 1) for i in range(count)]


def pair_high(count):
    return [(i, (i + 1 if i % 2 else i - 1) % count) for i in range(count)]


def shards(v):
    nx, nz = lax.axis_size("gx"), lax.axis_size("gz")
    v = pltpu.with_memory_space_constraint(v, pltpu.HBM)
    sems = [pltpu.SemaphoreType.DMA((CHUNKS,))]
    part_shape = pltpu.VMEM((3, X, Y, Z), F32)
    zb, za, xb, xa, vp, part = pl.pallas_call(
        pack_kernel,
        out_shape=[shape(208, Z), shape(200, Z)] + [shape(3, 2, Y, Z)] * 2 + [shape(3, X, WIDE, Z), part_shape],
        in_specs=[HBM],
        out_specs=[VM] * 6,
        scratch_shapes=[pltpu.SemaphoreType.DMA((LOADS,))],
        compiler_params=params(16),
        name="pack",
    )(v)
    rzb = lax.ppermute(zb, "gz", pair_high(nz))
    part, za = pl.pallas_call(
        second_kernel,
        out_shape=[part_shape, shape(200, Z)],
        in_specs=[VM] * 3,
        out_specs=[VM] * 2,
        input_output_aliases={1: 0},
        compiler_params=params(16),
        cost_estimate=COST,
        name="second",
    )(vp, part, za)
    rza = lax.ppermute(za, "gz", pair_low(nz))
    rxb = lax.ppermute(xb, "gx", pair_high(nx))
    rxa = lax.ppermute(xa, "gx", pair_low(nx))
    part = pl.pallas_call(
        third_kernel,
        out_shape=part_shape,
        in_specs=[VM] * 2,
        out_specs=VM,
        input_output_aliases={1: 0},
        compiler_params=params(16),
        cost_estimate=COST,
        name="third",
    )(vp, part)
    n, w, r, sums, edge, stored = pl.pallas_call(
        stencil_kernel,
        out_shape=[part_shape] * 3 + [shape(2, 3, Y, Z), shape(2, 3 * Y, Z), shape(3, X, Y, Z)],
        in_specs=[VM] * 6,
        out_specs=[VM] * 5 + [HBM],
        scratch_shapes=[pltpu.SemaphoreType.DMA(())],
        compiler_params=params(16),
        cost_estimate=COST,
        name="stencil",
    )(vp, part, za, zb, rzb, rza)
    n_ends, w_ends, r_ends, start, mom = pl.pallas_call(
        ends_kernel,
        out_shape=[shape(3, 4, Y, Z)] * 3 + [shape(3, Y, Z), shape(2, 3, Y, Z)],
        in_specs=[VM] * 5,
        out_specs=[VM] * 5,
        compiler_params=params(16),
        name="ends",
    )(vp, edge, sums, rxb, rxa)
    other = lax.ppermute(mom, "gx", pair_low(nx))
    half_cost = pl.CostEstimate(flops=0, bytes_accessed=4_000_000, transcendentals=0)
    stored = pl.pallas_call(
        store_first_kernel,
        out_shape=shape(3, X, Y, Z),
        in_specs=[VM, VM, HBM],
        out_specs=HBM,
        input_output_aliases={2: 0},
        scratch_shapes=[pltpu.SemaphoreType.DMA((2,))],
        compiler_params=params(8),
        cost_estimate=half_cost,
        name="store_first",
    )(n, n_ends, stored)
    stored = pltpu.with_memory_space_constraint(stored, pltpu.HBM)
    half = (2, 3, Y // 2, Z)
    chip = pl.pallas_call(
        chip_kernel,
        out_shape=shape(CHIPS, *half),
        in_specs=[VM, VM, HBM],
        out_specs=VM,
        compiler_params=params(16),
        name="chip",
    )(mom, other, stored)
    groups = [[core + 2 * k for k in range(CHIPS)] for core in range(2)]
    everyone = lax.all_to_all(chip, "gx", 0, 0, axis_index_groups=groups)
    joined = pl.pallas_call(
        join_kernel,
        out_shape=shape(*half),
        in_specs=[VM],
        out_specs=VM,
        compiler_params=params(16),
        name="join",
    )(everyone)
    joined_other = lax.ppermute(joined, "gx", pair_low(nx))
    stored = pl.pallas_call(
        store_last_kernel,
        out_shape=shape(3, X, Y, Z),
        in_specs=[VM, VM, HBM],
        out_specs=HBM,
        input_output_aliases={2: 0},
        scratch_shapes=[pltpu.SemaphoreType.DMA((2,))],
        compiler_params=params(8),
        cost_estimate=half_cost,
        name="store_last",
    )(n, n_ends, stored)
    new = pl.pallas_call(
        final_kernel,
        out_shape=shape(3, X, Y, Z),
        in_specs=[VM] * 8,
        out_specs=ANY,
        scratch_shapes=[pltpu.VMEM((3, X, Y, Z), F32), pltpu.SemaphoreType.DMA((GROUPS + 2,))],
        compiler_params=params(16),
        name="final",
    )(w, r, w_ends, r_ends, start, joined, joined_other, other)
    return new, stored


def solution(mesh):
    spec = P(None, "gx", None, "gz")
    return jax.shard_map(shards, mesh=mesh, in_specs=(spec,), out_specs=(spec, spec), check_vma=False)
```
